32 devices in a mesh: dp: 8 (over z, y), seq: 4 (over x, core).
Axes of the slice: x: 2, y: 2, z: 4, core: 2. Of those that a mesh axis runs over, the one named last changes fastest.
Arguments:
- frames: bfloat16 [4096, 1536], P('dp', 'seq')
- owner_slot: int32 [4096], P('dp'), may hold values from -1 to 4095, as said below
- segment: int32 [8, 512], P('dp'), may hold values from 0 to 2, never falling along the last dimension, each value on 1 to 256 neighbouring positions
- norm_gain: float32 [1536], replicated, may hold values from 0.25 to 1.75
- expand: bfloat16 [1536, 2, 1536], P('dp', None, 'seq'), may hold values from -0.15625 to 0.15625
- kernel: float32 [9, 1536], P(None, 'seq'), may hold values from -2.5 to 2.5
- project: bfloat16 [1536, 1536], P('seq', 'dp'), may hold values from -0.15625 to 0.15625
- cotangent: bfloat16 [4096, 1536], P('dp', 'seq'), may hold values from -6 to 6
Outputs:
- output: bfloat16 [4096, 1536], P('dp', 'seq')
- grad_frames: bfloat16 [4096, 1536], P('dp', 'seq')
- grad_gain: float32 [1536], P('seq')
- grad_kernel: float32 [9, 1536], P(None, 'seq')
- grad_expand: float32 [1536, 2, 1536], P('dp', None, 'seq')
- grad_project: float32 [1536, 1536], P('seq', 'dp')
The draws below stay inside these ranges and needn't reach their ends.
Inputs may be any that keep to these rules, and one draw needn't show every extreme that they name: `owner_slot`: for each arrival row, the balanced row that takes it, or -1 for an empty arrival row; no balanced row is named twice. The live rows of each pack come first, contiguous, ordered by sending index of dp and then by arrival row; empty rows fill the pack's tail. Of the 512 arrival rows of one index of dp, at most 64 name rows of any one pack; some pack takes exactly 64 rows from every index of dp. `segment`: within each pack the utterance numbers never fall; a pack holds 3 utterances of 1 to 256 frames, one of exactly 256.
All inputs are finite; a program needn't handle non-finite values.
Results may differ from the reference program's by a relative error of at most 0.01.
Values may be sent and summed in bfloat16 or wider, within the bound.
A program may use at most 128 MiB of HBM per device.

```python
import math
import jax
import jax.numpy as jnp
import numpy as np
from jax import lax

D = 1536
KSIZE = 9
USEG = 3
ROWS = 512
PACKS = 8
CAP = 64
ROWS_ALL = 4096
MOST_LEN = 256
N_SEQ = 4


def draw_frames(key, part):
    base_key, scale_key = jax.random.split(jax.random.fold_in(key, 3), 2)
    column_scale = jnp.exp(jax.random.uniform(scale_key, (1, D), jnp.float32, 0.0, math.log(10.0)))
    values = jax.random.normal(base_key, (ROWS_ALL, D), jnp.float32)
    return (0.3 * values * column_scale).astype(jnp.bfloat16)


def draw_owner_slot(key, part):
    count_key, full_key, source_key = jax.random.split(jax.random.fold_in(key, 7), 3)
    counts = jax.random.randint(count_key, (PACKS, PACKS), 0, CAP + 1)
    full_pack = jax.random.randint(full_key, (), 0, PACKS)
    counts = jnp.where(jnp.arange(PACKS)[None, :] == full_pack, CAP, counts)
    source_order = jax.vmap(lambda subkey: jax.random.permutation(subkey, ROWS))(jax.random.split(source_key, PACKS))
    bucket = source_order // CAP
    within = source_order % CAP
    sender = jnp.arange(PACKS)[:, None]
    alive_row = within < counts[sender, bucket]
    picks = (bucket[:, :, None] == jnp.arange(PACKS)[None, None, :]) & alive_row[:, :, None]
    picks = picks.astype(jnp.int32)
    before = jnp.cumsum(picks, axis=1) - picks
    rank = jnp.sum(before * picks, axis=2)
    offsets = jnp.cumsum(counts, axis=0) - counts
    landing = offsets[sender, bucket] + rank
    return jnp.where(alive_row, bucket * ROWS + landing, -1).astype(jnp.int32).reshape(ROWS_ALL)


def shard_levels(key, dims, cuts, least, top_value):
    gain, own = 1.0, jax.random.fold_in(key, 6)
    for axis_at, blocks in cuts:
        heights = jnp.exp(jax.random.uniform(jax.random.fold_in(own, axis_at), (blocks,), jnp.float32, least / len(cuts), top_value / len(cuts)))
        gain = gain * jnp.repeat(heights, dims[axis_at] // blocks).reshape([-1 if axis == axis_at else 1 for axis in range(len(dims))])
    return gain


def split_up(count, total, limit, lean):
    portions = [(1 << 20) // math.isqrt(standing ** lean) + 1 for standing in range(2, count + 1)]
    surplus, given = total - limit - (count - 1), [1] * (count - 1)
    while surplus > 0:
        free = [i for i in range(count - 1) if given[i] < limit]
        mass, budget = sum([portions[i] for i in free]), surplus
        for i in free:
            extra = min(limit - given[i], max(1, budget * portions[i] // mass), surplus)
            given[i] = given[i] + extra
            surplus = surplus - extra
    return np.array([limit] + given)


def uneven_parts(own_key, amount, total, most, skew):
    if amount == 2:
        one = jax.random.randint(own_key, (), max(1, total - most), min(most, total - 1) + 1)
        return jnp.stack([one, total - one])
    lengths = jnp.asarray(split_up(amount, total, most, skew), jnp.int32)
    pairs = (amount - 1) // 2
    giver, receiver = lengths[1:1 + 2 * pairs:2], lengths[2:2 + 2 * pairs:2]
    room = jnp.minimum(giver - 1, most - receiver)
    shifted = jax.random.randint(jax.random.fold_in(own_key, 1), (pairs,), 0, 1 << 20) % (room + 1)
    lengths = lengths.at[1:1 + 2 * pairs:2].set(giver - shifted).at[2:2 + 2 * pairs:2].set(receiver + shifted)
    return lengths[jax.random.permutation(jax.random.fold_in(own_key, 2), amount)]


def noise(stream_key, dims, deviation, reach, cuts=(), dtype=jnp.bfloat16):
    level = shard_levels(stream_key, dims, cuts, -0.22, 0.18) if cuts else 1.0
    entries = jax.random.normal(stream_key, dims, jnp.float32) * deviation * level
    return jnp.minimum(jnp.maximum(entries, -reach), reach).astype(dtype)


def setup_inputs(seed: int = 0) -> dict:
    key_of = jax.random.split(jax.random.key(seed), 9)
    return {
        "frames": draw_frames(jax.random.fold_in(key_of[8], 71), 0),
        "owner_slot": draw_owner_slot(jax.random.fold_in(key_of[8], 71), 0),
        "segment": jax.vmap(lambda own: jnp.searchsorted(jnp.cumsum(uneven_parts(own, USEG, ROWS, MOST_LEN, 2)), jnp.arange(ROWS), side="right"))(jax.random.split(key_of[2], PACKS)).reshape((PACKS, ROWS)).astype(jnp.int32),
        "norm_gain": jnp.clip(1.0 + 0.15 * jax.random.normal(key_of[3], (D,), jnp.float32), 0.25, 1.75),
        "expand": noise(key_of[4], (D, 2, D), D ** -0.5, 0.15625, ((0, 8), (2, 4))),
        "kernel": noise(key_of[5], (KSIZE, D), 5 ** -0.5, 2.5, ((1, 4),), jnp.float32),
        "project": noise(key_of[6], (D, D), D ** -0.5, 0.15625, ((0, 4), (1, 8))),
        "cotangent": noise(key_of[7], (ROWS_ALL, D), 1.0, 6.0, ((0, 8), (1, 4))),
    }


EPS = 1e-05

def conv_masks(labels):
    half_width = (KSIZE - 1) // 2
    length = labels.shape[0]
    padded = jnp.pad(labels, (half_width, half_width), constant_values=-1)
    return [(padded[tap_index:tap_index + length] == labels).astype(jnp.float32)[:, None] for tap_index in range(KSIZE)]

def depthwise(signal, kernel, tap_masks):
    half_width = (KSIZE - 1) // 2
    length = signal.shape[0]
    padded = jnp.pad(signal, ((half_width, half_width), (0, 0)))
    total = jnp.zeros(signal.shape, jnp.float32)
    for tap_index in range(KSIZE):
        total = total + kernel[tap_index] * padded[tap_index:tap_index + length] * tap_masks[tap_index]
    return total

def depthwise_back(signal, upstream, kernel, tap_masks):
    half_width = (KSIZE - 1) // 2
    length = signal.shape[0]
    padded = jnp.pad(signal, ((half_width, half_width), (0, 0)))
    spread = jnp.zeros((length + 2 * half_width, signal.shape[1]), jnp.float32)
    tap_sums = []
    for tap_index in range(KSIZE):
        masked = upstream * tap_masks[tap_index]
        tap_sums.append(lax.optimization_barrier(jnp.sum(masked * padded[tap_index:tap_index + length], axis=0)))
        spread = spread + jnp.pad(kernel[tap_index] * masked, ((tap_index, 2 * half_width - tap_index), (0, 0)))
    return (jnp.stack(tap_sums), spread[half_width:half_width + length])

def reference(frames, owner_slot, segment, norm_gain, expand, kernel, project, cotangent):
    target = jnp.where(owner_slot >= 0, owner_slot, ROWS_ALL).astype(jnp.int32)
    packed = jnp.zeros((ROWS_ALL, D), jnp.bfloat16).at[target].set(frames, mode='drop')
    live_rows = jnp.zeros((ROWS_ALL,), jnp.float32).at[target].set(1.0, mode='drop')
    quarter = D // N_SEQ
    expand_flat = expand.reshape(D, 2 * D)
    inv_root = 1.0 / math.sqrt(ROWS_ALL)

    def one_pack(totals, inputs):
        pack_rows, pack_live, labels, cot_rows = inputs
        live_col = pack_live[:, None]
        tap_masks = conv_masks(labels)
        floats = pack_rows.astype(jnp.float32)
        row_mean = lax.optimization_barrier(jnp.mean(floats, axis=1, keepdims=True))
        centred = floats - row_mean
        inv_scale = lax.rsqrt(lax.optimization_barrier(jnp.mean(centred * centred, axis=1, keepdims=True)) + EPS)
        normed = centred * inv_scale
        scaled = (normed * norm_gain).astype(jnp.bfloat16)
        joined = jnp.dot(scaled, expand_flat, preferred_element_type=jnp.float32)
        value_half = joined[:, :D]
        gate_sig = jax.nn.sigmoid(joined[:, D:])
        glu_out = value_half * gate_sig
        conv_out = depthwise(glu_out, kernel, tap_masks)
        conv_sig = jax.nn.sigmoid(conv_out)
        hidden = (conv_out * conv_sig * live_col).astype(jnp.bfloat16)
        mixed_total = jnp.zeros((ROWS, D), jnp.float32)
        for lane_pos in range(N_SEQ):
            lane_cols = slice(lane_pos * quarter, (lane_pos + 1) * quarter)
            part_out = jnp.dot(hidden[:, lane_cols], project[lane_cols], preferred_element_type=jnp.float32)
            mixed_total = mixed_total + lax.optimization_barrier(part_out.astype(jnp.bfloat16)).astype(jnp.float32)
        output = (floats + mixed_total).astype(jnp.bfloat16)
        project_term = jnp.dot(hidden.T, cot_rows, preferred_element_type=jnp.float32)
        hidden_grad = jnp.dot(cot_rows, project.T, preferred_element_type=jnp.float32) * live_col
        conv_grad = hidden_grad * (conv_sig + conv_out * conv_sig * (1.0 - conv_sig))
        kernel_term, glu_grad = depthwise_back(glu_out, conv_grad, kernel, tap_masks)
        proj_grad = jnp.stack([glu_grad * gate_sig, glu_grad * value_half * gate_sig * (1.0 - gate_sig)], axis=1).astype(jnp.bfloat16)
        expand_term = jnp.dot(scaled.T, proj_grad.reshape(ROWS, 2 * D), preferred_element_type=jnp.float32)
        scaled_grad = jnp.zeros((ROWS, D), jnp.float32)
        for lane_pos in range(N_SEQ):
            lane_cols = slice(lane_pos * quarter, (lane_pos + 1) * quarter)
            grad_block = proj_grad[:, :, lane_cols].reshape(ROWS, 2 * quarter)
            weight_block = expand[:, :, lane_cols].reshape(D, 2 * quarter)
            part_grad = jnp.dot(grad_block, weight_block.T, preferred_element_type=jnp.float32)
            scaled_grad = scaled_grad + lax.optimization_barrier(part_grad.astype(jnp.bfloat16)).astype(jnp.float32)
        normed_grad = scaled_grad * norm_gain
        first_mean = lax.optimization_barrier(jnp.mean(normed_grad, axis=1, keepdims=True))
        second_mean = lax.optimization_barrier(jnp.mean(normed_grad * normed, axis=1, keepdims=True))
        packed_grad = inv_scale * (normed_grad - first_mean - normed * second_mean) + cot_rows.astype(jnp.float32)
        gain_term = lax.optimization_barrier(jnp.sum(scaled_grad * normed, axis=0))
        totals = (totals[0] + gain_term, totals[1] + kernel_term, totals[2] + expand_term, totals[3] + project_term)
        return (totals, (output, packed_grad.astype(jnp.bfloat16)))
    start_totals = (jnp.zeros((D,), jnp.float32), jnp.zeros((KSIZE, D), jnp.float32), jnp.zeros((D, 2 * D), jnp.float32), jnp.zeros((D, D), jnp.float32))
    totals, stacked = lax.scan(one_pack, start_totals, (packed.reshape(PACKS, ROWS, D), live_rows.reshape(PACKS, ROWS), segment, cotangent.reshape(PACKS, ROWS, D)))
    output = stacked[0].reshape(ROWS_ALL, D)
    packed_grad = stacked[1].reshape(ROWS_ALL, D)
    safe_slot = jnp.maximum(owner_slot, 0).astype(jnp.int32)
    grad_frames = jnp.where((owner_slot >= 0)[:, None], packed_grad[safe_slot], jnp.zeros((), jnp.bfloat16))
    grad_gain = totals[0] * inv_root
    grad_kernel = totals[1] * inv_root
    grad_expand = totals[2].reshape(D, 2, D) * inv_root
    grad_project = totals[3] * inv_root
    return (output, grad_frames, grad_gain, grad_kernel, grad_expand, grad_project)
```

```python
import functools
import math

import jax
import jax.numpy as jnp
from jax import lax
from jax.experimental import pallas as pl
from jax.experimental.pallas import tpu as pltpu
from jax.sharding import PartitionSpec as P

D = 1536
KSIZE = 9
HALF = KSIZE // 2
EPS = 1e-05
BF16 = jnp.bfloat16
F32 = jnp.float32
NT = (((1,), (1,)), ((), ()))
TN = (((0,), (0,)), ((), ()))


def dot(a, b, dims=(((1,), (0,)), ((), ())), precision=None):
    return lax.dot_general(a, b, dims, preferred_element_type=F32, precision=precision)


def span(index, size):
    return pl.ds(pl.multiple_of(index * size, size), size)


def enter(groups, lanes):
    me, lane = lax.axis_index("dp"), lax.axis_index("seq")
    barrier = pltpu.get_barrier_semaphore()

    def greet_group(k, carry):
        pl.semaphore_signal(barrier, inc=1, device_id=(lax.rem(me + k, groups), lane),
                            device_id_type=pl.DeviceIdType.MESH)
        return carry

    def greet_lane(k, carry):
        pl.semaphore_signal(barrier, inc=1, device_id=(me, lax.rem(lane + k, lanes)),
                            device_id_type=pl.DeviceIdType.MESH)
        return carry

    lax.fori_loop(1, groups, greet_group, 0)
    lax.fori_loop(1, lanes, greet_lane, 0)
    pl.semaphore_wait(barrier, groups + lanes - 2)


def remote(src, dst, sems, k, device):
    return pltpu.make_async_remote_copy(
        src_ref=src, dst_ref=dst, send_sem=sems.at[0, k], recv_sem=sems.at[1, k],
        device_id=device, device_id_type=pl.DeviceIdType.MESH)


def each(first, last, body):
    def step(k, carry):
        body(k)
        return carry

    lax.fori_loop(first, last, step, 0)


def arrive_kernel(groups, lanes, cap,
                  owner_ref, frames_ref, weight_ref, cot_ref,
                  local_ref, whole_ref, cot_full_ref, weight_full_ref, pick_ref, place_ref, total_ref,
                  outgoing, incoming, owners, row_sem, owner_sem, outer_sem, pair_sem, cot_sem, whole_sem, own_sem):
    rows, quarter = frames_ref.shape
    me, lane = lax.axis_index("dp"), lax.axis_index("seq")
    outers = groups // 2
    outer, inner = me // 2, lax.rem(me, 2)
    mate = outer * 2 + 1 - inner
    enter(groups, lanes)

    def owner_copy(k):
        return remote(owner_ref, owners.at[me], owner_sem, k, (lax.rem(me + k, groups), lane))

    def row_copy(k):
        to = lax.rem(me + k, groups)
        return remote(outgoing.at[to], incoming.at[me], row_sem, k, (to, lane))

    def outer_copy(k):
        to = lax.rem(outer + k, outers) * 2 + inner
        return remote(weight_ref, weight_full_ref.at[me], outer_sem, k, (to, lane))

    def pair_copy(k):
        held = lax.rem(outer - k + outers, outers) * 2 + inner
        return remote(weight_full_ref.at[held], weight_full_ref.at[held], pair_sem, k, (mate, lane))

    def first_pair_copy():
        return remote(weight_ref, weight_full_ref.at[me], pair_sem, 0, (mate, lane))

    def cot_copy(k):
        return remote(cot_ref, cot_full_ref.at[:, span(lane, quarter)], cot_sem, k,
                      (me, lax.rem(lane + k, lanes)))

    def whole_copy(k):
        return remote(local_ref, whole_ref.at[:, span(lane, quarter)], whole_sem, k,
                      (me, lax.rem(lane + k, lanes)))

    each(1, groups, lambda k: owner_copy(k).start())
    own_weight = pltpu.make_async_copy(weight_ref, weight_full_ref.at[me], own_sem.at[0])
    own_weight.start()
    own_cot = pltpu.make_async_copy(cot_ref, cot_full_ref.at[:, span(lane, quarter)], own_sem.at[1])
    own_cot.start()

    slot = owner_ref[0:1, :]
    group_id = lax.broadcasted_iota(jnp.int32, (groups, rows), 0)
    named = jnp.where((slot >= group_id * rows) & (slot < group_id * rows + rows), 1.0, 0.0)
    before = jnp.where(lax.broadcasted_iota(jnp.int32, (rows, rows), 0)
                       < lax.broadcasted_iota(jnp.int32, (rows, rows), 1), 1.0, 0.0).astype(BF16)
    rank = dot(named.astype(BF16), before)
    base = group_id.astype(F32) * cap
    position = jnp.sum((rank + base + 1.0) * named, axis=0, keepdims=True) - 1.0
    slots = groups * cap
    pick = jnp.where(lax.broadcasted_iota(jnp.int32, (slots, rows), 0) == position.astype(jnp.int32), 1.0, 0.0).astype(BF16)
    pick_ref[...] = pick
    outgoing[...] = dot(pick, frames_ref[...]).astype(BF16).reshape(groups, cap, quarter)
    each(1, groups, lambda k: row_copy(k).start())
    first_pair_copy().start()
    each(1, outers, lambda k: outer_copy(k).start())
    each(1, lanes, lambda k: cot_copy(k).start())

    owners[me] = owner_ref[...]
    incoming[me] = outgoing[me]
    each(1, groups, lambda k: owner_copy(k).wait())
    mine = lax.broadcasted_iota(jnp.int32, (1, rows), 1) * 0 + me * rows
    total = jnp.zeros((1, 1), F32)
    row_id = lax.broadcasted_iota(jnp.int32, (cap, rows), 1).astype(F32)
    step_id = lax.broadcasted_iota(jnp.int32, (cap, rows), 0).astype(F32)
    for source in range(groups):
        theirs = owners[source][0:1, :]
        count = jnp.sum(jnp.where((theirs >= mine) & (theirs < mine + rows), 1.0, 0.0), axis=1, keepdims=True)
        hit = (row_id - step_id == total) & (step_id < count)
        place_ref[pl.ds(source * cap, cap), :] = jnp.where(hit, 1.0, 0.0).astype(BF16)
        total = total + count
    total_ref[...] = jnp.broadcast_to(total, total_ref.shape)
    each(1, groups, lambda k: row_copy(k).wait())
    local_ref[...] = dot(place_ref[...], incoming[...].reshape(slots, quarter), TN).astype(BF16)
    own_whole = pltpu.make_async_copy(local_ref, whole_ref.at[:, span(lane, quarter)], own_sem.at[2])
    own_whole.start()
    each(1, lanes, lambda k: whole_copy(k).start())

    def forward(k):
        outer_copy(k).wait_recv()
        pair_copy(k).start()

    each(1, outers, forward)
    each(1, outers, lambda k: outer_copy(k).wait_send())
    first_pair_copy().wait()
    each(1, outers, lambda k: pair_copy(k).wait())
    each(1, lanes, lambda k: cot_copy(k).wait())
    each(1, lanes, lambda k: whole_copy(k).wait())
    own_weight.wait()
    own_cot.wait()
    own_whole.wait()


def leave_kernel(groups, lanes, cap, scale,
                 terms_ref, scaled_ref, mixed_ref, tap_ref, cot_ref, normed_ref, inv_ref, gain_ref, local_ref, pick_ref, place_ref,
                 out_ref, frames_ref, small_ref, weight_ref,
                 pair_in, pair_sum, outer_in, scaled_in, mixed_in, small_in, small_out, sums_in, sums_out, returning, returned,
                 pair_sem, outer_sem, scaled_sem, mixed_sem, small_sem, sums_sem, row_sem):
    rows, quarter = local_ref.shape
    me, lane = lax.axis_index("dp"), lax.axis_index("seq")
    outers = groups // 2
    outer, inner = me // 2, lax.rem(me, 2)
    mate = outer * 2 + 1 - inner
    slots = groups * cap
    enter(groups, lanes)

    def pair_copy(k):
        at = lax.rem(outer + k, outers)
        return remote(terms_ref.at[at * 2 + 1 - inner], pair_in.at[at], pair_sem, k, (mate, lane))

    def outer_copy(k):
        at = lax.rem(outer + k, outers)
        return remote(pair_sum.at[at], outer_in.at[outer], outer_sem, k, (at * 2 + inner, lane))

    def lane_copy(src, dst, sems, k):
        to = lax.rem(lane + k, lanes)
        return remote(src.at[:, span(to, quarter)], dst.at[lane], sems, k, (me, to))

    def sums_copy(k):
        return remote(sums_out, sums_in.at[lane], sums_sem, k, (me, lax.rem(lane + k, lanes)))

    def small_copy(k):
        return remote(small_out, small_in.at[me], small_sem, k, (lax.rem(me + k, groups), lane))

    def row_copy(k):
        to = lax.rem(me + k, groups)
        return remote(returning.at[to], returned.at[me], row_sem, k, (to, lane))

    each(1, lanes, lambda k: lane_copy(scaled_ref, scaled_in, scaled_sem, k).start())
    each(1, outers, lambda k: pair_copy(k).start())
    pair_copy(0).start()
    each(1, lanes, lambda k: lane_copy(mixed_ref, mixed_in, mixed_sem, k).start())

    def pass_on(k):
        pair_copy(k).wait_recv()
        at = lax.rem(outer + k, outers)
        pair_sum[at] = (terms_ref[at * 2 + inner].astype(F32) + pair_in[at].astype(F32)).astype(BF16)
        outer_copy(k).start()

    pass_on(1)

    scaled_in[lane] = scaled_ref[:, span(lane, quarter)]
    each(1, lanes, lambda k: lane_copy(scaled_ref, scaled_in, scaled_sem, k).wait())
    share = scaled_in[0].astype(F32)
    for k in range(1, lanes):
        share = share + scaled_in[k].astype(F32)
    normed = normed_ref[...]
    grown = share * gain_ref[...]
    ones = jnp.ones((8, quarter), F32)
    sums_out[0:8, :] = dot(ones, grown, NT, lax.Precision.HIGHEST)
    sums_out[8:16, :] = dot(ones, grown * normed, NT, lax.Precision.HIGHEST)
    each(1, lanes, lambda k: sums_copy(k).start())
    small_out[...] = tap_ref[...]
    small_out[KSIZE:KSIZE + 1, :] = jnp.sum(share * normed, axis=0, keepdims=True)
    each(1, groups, lambda k: small_copy(k).start())
    each(2, outers, pass_on)
    pair_copy(0).wait_recv()
    own = terms_ref[me].astype(F32) + pair_in[outer].astype(F32)
    sums_in[lane] = sums_out[...]
    each(1, lanes, lambda k: sums_copy(k).wait())
    sums = sums_in[0]
    for k in range(1, lanes):
        sums = sums + sums_in[k]
    means = jnp.transpose(sums) * (1.0 / (lanes * quarter))
    back = inv_ref[...] * (grown - means[:, 0:1] - normed * means[:, 8:9]) + cot_ref[...].astype(F32)
    returning[...] = dot(place_ref[...], back.astype(BF16)).astype(BF16).reshape(groups, cap, quarter)
    each(1, groups, lambda k: row_copy(k).start())

    mixed_in[lane] = mixed_ref[:, span(lane, quarter)]
    each(1, lanes, lambda k: lane_copy(mixed_ref, mixed_in, mixed_sem, k).wait())
    mixed = mixed_in[0].astype(F32)
    for k in range(1, lanes):
        mixed = mixed + mixed_in[k].astype(F32)
    out_ref[...] = (local_ref[...].astype(F32) + mixed).astype(BF16)

    small_in[me] = small_out[...]
    each(1, groups, lambda k: small_copy(k).wait())
    small = small_in[0]
    for k in range(1, groups):
        small = small + small_in[k]
    small_ref[...] = small * scale

    returned[me] = returning[me]
    each(1, groups, lambda k: row_copy(k).wait())
    frames_ref[...] = dot(pick_ref[...], returned[...].reshape(slots, quarter), TN).astype(BF16)

    weight_ref[...] = own

    def add_up(k):
        outer_copy(k).wait_recv()
        weight_ref[...] += outer_in[lax.rem(outer - k + outers, outers)].astype(F32)

    each(1, outers, add_up)
    weight_ref[...] = weight_ref[...] * scale
    each(1, outers, lambda k: outer_copy(k).wait_send())
    each(0, outers, lambda k: pair_copy(k).wait_send())


def conv_masks(labels):
    length = labels.shape[0]
    padded = jnp.pad(labels, (HALF, HALF), constant_values=-1)
    return [
        (padded[k : k + length] == labels).astype(F32)[:, None] for k in range(KSIZE)
    ]


def shards(frames, owner_slot, segment, norm_gain, expand, kernel, project, cotangent):
    rows, quarter = frames.shape
    groups, lanes = lax.axis_size("dp"), lax.axis_size("seq")
    lane = lax.axis_index("seq")
    cap = max(16, rows // groups)
    slots = groups * cap
    depth = D // groups
    wide = 3 * quarter
    inv_root = 1.0 / math.sqrt(rows * groups)
    vmem = pl.BlockSpec(memory_space=pltpu.VMEM)
    anywhere = pl.BlockSpec(memory_space=pl.ANY)
    dma = pltpu.SemaphoreType.DMA
    weight = jnp.concatenate([expand.reshape(depth, 2 * quarter), project.T], axis=1)
    owner_rows = jnp.broadcast_to(owner_slot[None, :], (8, rows))
    local_rows, whole_rows, cot_full, weight_full, pick, place, total = pl.pallas_call(
        functools.partial(arrive_kernel, groups, lanes, cap),
        out_shape=(
            jax.ShapeDtypeStruct((rows, quarter), BF16),
            jax.ShapeDtypeStruct((rows, D), BF16),
            jax.ShapeDtypeStruct((rows, D), BF16),
            jax.ShapeDtypeStruct((groups, depth, wide), BF16),
            jax.ShapeDtypeStruct((slots, rows), BF16),
            jax.ShapeDtypeStruct((slots, rows), BF16),
            jax.ShapeDtypeStruct((8, 128), F32),
        ),
        in_specs=[vmem, vmem, anywhere, anywhere],
        out_specs=(vmem, anywhere, anywhere, anywhere, vmem, vmem, vmem),
        scratch_shapes=[
            pltpu.VMEM((groups, cap, quarter), BF16),
            pltpu.VMEM((groups, cap, quarter), BF16),
            pltpu.VMEM((groups, 8, rows), jnp.int32),
            dma((2, groups)), dma((2, groups)), dma((2, groups // 2)), dma((2, groups // 2)),
            dma((2, lanes)), dma((2, lanes)), dma((3,)),
        ],
        compiler_params=pltpu.CompilerParams(collective_id=0, has_side_effects=True, vmem_limit_bytes=40 << 20),
        name="arrive",
    )(owner_rows, frames, weight, cotangent)
    weight_full = weight_full.reshape(D, wide)
    expand_full = weight_full[:, : 2 * quarter]
    project_back = weight_full[:, 2 * quarter :]
    live_col = (lax.broadcasted_iota(jnp.int32, (rows, 1), 0).astype(F32) < total[0, 0]).astype(F32)
    floats = whole_rows.astype(F32)
    row_mean = jnp.mean(floats, axis=1, keepdims=True)
    centred = floats - row_mean
    inv_scale = lax.rsqrt(jnp.mean(centred * centred, axis=1, keepdims=True) + EPS)
    scaled = (centred * inv_scale * norm_gain).astype(BF16)
    normed_local = (local_rows.astype(F32) - row_mean) * inv_scale
    joined = dot(scaled, expand_full)
    value_half = joined[:, :quarter]
    gate_sig = jax.nn.sigmoid(joined[:, quarter:])
    glu_out = value_half * gate_sig
    masks = conv_masks(segment[0])
    around = jnp.pad(glu_out, ((HALF, HALF), (0, 0)))
    conv_out = sum(kernel[k] * around[k : k + rows] * masks[k] for k in range(KSIZE))
    conv_sig = jax.nn.sigmoid(conv_out)
    hidden = (conv_out * conv_sig * live_col).astype(BF16)
    mixed_part = dot(hidden, project_back, NT).astype(BF16)
    hidden_grad = dot(cot_full, project_back) * live_col
    conv_grad = hidden_grad * (conv_sig + conv_out * conv_sig * (1.0 - conv_sig))
    upstream = jnp.pad(conv_grad, ((HALF, HALF), (0, 0)))
    glu_grad = sum(
        kernel[k] * upstream[2 * HALF - k : 2 * HALF - k + rows] * masks[KSIZE - 1 - k] for k in range(KSIZE)
    )
    taps = jnp.stack(
        [jnp.sum(conv_grad * around[k : k + rows] * masks[k], axis=0) for k in range(KSIZE)]
    )
    proj_grad = jnp.concatenate(
        [glu_grad * gate_sig, glu_grad * value_half * gate_sig * (1.0 - gate_sig)], axis=1
    ).astype(BF16)
    terms = jnp.concatenate([dot(scaled, proj_grad, TN).astype(BF16), dot(cot_full, hidden, TN).astype(BF16)], axis=1)
    scaled_part = dot(proj_grad, expand_full, NT).astype(BF16)
    gain_local = lax.dynamic_slice_in_dim(norm_gain, lane * quarter, quarter, 0)[None, :]
    output, grad_frames, small, weight_grad = pl.pallas_call(
        functools.partial(leave_kernel, groups, lanes, cap, inv_root),
        out_shape=(
            jax.ShapeDtypeStruct((rows, quarter), BF16),
            jax.ShapeDtypeStruct((rows, quarter), BF16),
            jax.ShapeDtypeStruct((16, quarter), F32),
            jax.ShapeDtypeStruct((depth, wide), F32),
        ),
        in_specs=[vmem] * 11,
        out_specs=(vmem,) * 4,
        scratch_shapes=[
            pltpu.VMEM((groups // 2, depth, wide), BF16),
            pltpu.VMEM((groups // 2, depth, wide), BF16),
            pltpu.VMEM((groups // 2, depth, wide), BF16),
            pltpu.VMEM((lanes, rows, quarter), BF16),
            pltpu.VMEM((lanes, rows, quarter), BF16),
            pltpu.VMEM((groups, 16, quarter), F32),
            pltpu.VMEM((16, quarter), F32),
            pltpu.VMEM((lanes, 16, rows), F32),
            pltpu.VMEM((16, rows), F32),
            pltpu.VMEM((groups, cap, quarter), BF16),
            pltpu.VMEM((groups, cap, quarter), BF16),
            dma((2, groups // 2)), dma((2, groups // 2)), dma((2, lanes)), dma((2, lanes)),
            dma((2, groups)), dma((2, lanes)), dma((2, groups)),
        ],
        compiler_params=pltpu.CompilerParams(collective_id=1, has_side_effects=True, vmem_limit_bytes=48 << 20),
        name="leave",
    )(
        terms.reshape(groups, depth, wide), scaled_part, mixed_part, jnp.pad(taps, ((0, 16 - KSIZE), (0, 0))),
        cotangent, normed_local, inv_scale, gain_local, local_rows, pick, place,
    )
    return (
        output,
        grad_frames,
        small[KSIZE],
        small[:KSIZE],
        weight_grad[:, : 2 * quarter].reshape(depth, 2, quarter),
        weight_grad[:, 2 * quarter :].T,
    )


def solution(mesh):
    placed = (
        P("dp", "seq"),
        P("dp"),
        P("dp", None),
        P(),
        P("dp", None, "seq"),
        P(None, "seq"),
        P("seq", "dp"),
        P("dp", "seq"),
    )
    return jax.shard_map(
        shards,
        mesh=mesh,
        in_specs=placed,
        out_specs=(
            P("dp", "seq"),
            P("dp", "seq"),
            P("seq"),
            P(None, "seq"),
            P("dp", None, "seq"),
            P("seq", "dp"),
        ),
        check_vma=False,
    )
```

```python
import functools
import math

import jax
import jax.numpy as jnp
from jax import lax
from jax.experimental import pallas as pl
from jax.experimental.pallas import tpu as pltpu
from jax.sharding import PartitionSpec as P

D = 1536
KSIZE = 9
HALF = KSIZE // 2
EPS = 1e-05
BF16 = jnp.bfloat16
F32 = jnp.float32
NT = (((1,), (1,)), ((), ()))
TN = (((0,), (0,)), ((), ()))


def dot(a, b, dims=(((1,), (0,)), ((), ())), precision=None):
    return lax.dot_general(a, b, dims, preferred_element_type=F32, precision=precision)


def span(index, size):
    return pl.ds(pl.multiple_of(index * size, size), size)


def enter(groups, lanes):
    me, lane = lax.axis_index("dp"), lax.axis_index("seq")
    barrier = pltpu.get_barrier_semaphore()

    def greet_group(k, carry):
        pl.semaphore_signal(barrier, inc=1, device_id=(lax.rem(me + k, groups), lane),
                            device_id_type=pl.DeviceIdType.MESH)
        return carry

    def greet_lane(k, carry):
        pl.semaphore_signal(barrier, inc=1, device_id=(me, lax.rem(lane + k, lanes)),
                            device_id_type=pl.DeviceIdType.MESH)
        return carry

    lax.fori_loop(1, groups, greet_group, 0)
    lax.fori_loop(1, lanes, greet_lane, 0)
    pl.semaphore_wait(barrier, groups + lanes - 2)


def remote(src, dst, sems, k, device):
    return pltpu.make_async_remote_copy(
        src_ref=src, dst_ref=dst, send_sem=sems.at[0, k], recv_sem=sems.at[1, k],
        device_id=device, device_id_type=pl.DeviceIdType.MESH)


def each(first, last, body):
    def step(k, carry):
        body(k)
        return carry

    lax.fori_loop(first, last, step, 0)


def flat(parts):
    n, rows, columns = parts.shape
    if rows % 16:
        return parts.astype(F32).reshape(n * rows, columns).astype(BF16)
    return parts.reshape(n * rows, columns)


def sigmoid(x):
    return 1.0 / (1.0 + jnp.exp(-x))


def block_kernel(groups, lanes, cap, scale,
                 owner_ref, frames_ref, expand_ref, project_ref, cot_ref, gain_ref, gain_local_ref, taps_ref, mask_ref,
                 out_ref, back_ref, small_ref, grad_expand_ref, grad_project_ref,
                 outgoing, incoming, owners, pick, place, local, whole, cot_full, scaled, expand_full, project_full,
                 around, upstream, conv, value, gate, mixed_part, scaled_part,
                 expand_terms, expand_in, expand_sum, expand_last, project_terms, project_in, project_sum, project_last,
                 scaled_in, mixed_in, small_in, small_out, sums_in, sums_out, returning, returned,
                 owner_sem, row_sem, cot_sem, whole_sem, eo_sem, ep_sem, po_sem, pp_sem,
                 ge_pair, ge_outer, gp_pair, gp_outer, scaled_sem, mixed_sem, small_sem, sums_sem, back_sem):
    rows, quarter = frames_ref.shape
    depth = expand_ref.shape[0]
    me, lane = lax.axis_index("dp"), lax.axis_index("seq")
    outers = groups // 2
    outer, inner = me // 2, lax.rem(me, 2)
    mate = outer * 2 + 1 - inner
    high, low = lane // 2, lax.rem(lane, 2)
    sibling = high * 2 + 1 - low
    opposite = lax.rem(lane + 2, lanes)
    slots = groups * cap
    enter(groups, lanes)

    def to_group(src, dst, sems):
        def copy(k):
            return remote(src, dst.at[me], sems, k, (lax.rem(me + k, groups), lane))
        return copy

    def rows_to_group(src, dst, sems):
        def copy(k):
            to = lax.rem(me + k, groups)
            return remote(src.at[to], dst.at[me], sems, k, (to, lane))
        return copy

    def lane_gather(buffer, sems):
        own, far = buffer.at[:, span(lane, quarter)], buffer.at[:, span(opposite, quarter)]
        return (remote(own, own, sems, 0, (me, opposite)), remote(own, own, sems, 1, (me, sibling)),
                remote(far, far, sems, 2, (me, sibling)))

    def lane_scatter(src, dst, sems):
        def copy(k):
            to = lax.rem(lane + k, lanes)
            return remote(src.at[:, span(to, quarter)], dst.at[lane], sems, k, (me, to))
        return copy

    def gather_outer(full, sems):
        def copy(k):
            return remote(full.at[me], full.at[me], sems, k, (lax.rem(outer + k, outers) * 2 + inner, lane))
        return copy

    def gather_pair(full, sems):
        def copy(k):
            held = lax.rem(outer - k + outers, outers) * 2 + inner
            return remote(full.at[held], full.at[held], sems, k, (mate, lane))
        return copy

    def term_pair(terms, landing, sems):
        def copy(k):
            at = lax.rem(outer + k, outers)
            return remote(terms.at[at * 2 + 1 - inner], landing.at[at], sems, k, (mate, lane))
        return copy

    def term_outer(summed, landing, sems):
        def copy(k):
            at = lax.rem(outer + k, outers)
            return remote(summed.at[at], landing.at[outer], sems, k, (at * 2 + inner, lane))
        return copy

    owner_copy = to_group(owner_ref, owners, owner_sem)
    row_copy = rows_to_group(outgoing, incoming, row_sem)
    cot_copies = lane_gather(cot_full, cot_sem)
    whole_copies = lane_gather(whole, whole_sem)
    expand_outer, expand_pair = gather_outer(expand_full, eo_sem), gather_pair(expand_full, ep_sem)
    project_outer, project_pair = gather_outer(project_full, po_sem), gather_pair(project_full, pp_sem)
    mixed_copy = lane_scatter(mixed_part, mixed_in, mixed_sem)
    scaled_copy = lane_scatter(scaled_part, scaled_in, scaled_sem)
    gp_first, gp_second = term_pair(project_terms, project_in, gp_pair), term_outer(project_sum, project_last, gp_outer)
    ge_first, ge_second = term_pair(expand_terms, expand_in, ge_pair), term_outer(expand_sum, expand_last, ge_outer)
    small_copy = to_group(small_out, small_in, small_sem)
    back_copy = rows_to_group(returning, returned, back_sem)

    def sums_copy(k):
        return remote(sums_out, sums_in.at[lane], sums_sem, k, (me, lax.rem(lane + k, lanes)))

    each(1, groups, lambda k: owner_copy(k).start())
    slot = owner_ref[0:1, :]
    group_id = lax.broadcasted_iota(jnp.int32, (groups, rows), 0)
    named = jnp.where((slot >= group_id * rows) & (slot < group_id * rows + rows), 1.0, 0.0)
    before = jnp.where(lax.broadcasted_iota(jnp.int32, (rows, rows), 0)
                       < lax.broadcasted_iota(jnp.int32, (rows, rows), 1), 1.0, 0.0).astype(BF16)
    rank = dot(named.astype(BF16), before)
    position = jnp.sum((rank + group_id.astype(F32) * cap + 1.0) * named, axis=0, keepdims=True) - 1.0
    pick[...] = jnp.where(lax.broadcasted_iota(jnp.int32, (slots, rows), 0) == position.astype(jnp.int32), 1.0, 0.0).astype(BF16)
    outgoing[...] = dot(pick[...], frames_ref[...]).astype(BF16).reshape(groups, cap, quarter)
    each(1, groups, lambda k: row_copy(k).start())
    expand_full[me] = expand_ref[...]
    expand_pair(0).start()
    each(1, outers, lambda k: expand_outer(k).start())
    cot_full[:, span(lane, quarter)] = cot_ref[...]
    cot_copies[0].start()
    cot_copies[1].start()

    project_full[me] = project_ref[...]
    owners[me] = owner_ref[...]
    incoming[me] = outgoing[me]
    each(1, groups, lambda k: owner_copy(k).wait())
    mine = lax.broadcasted_iota(jnp.int32, (1, rows), 1) * 0 + me * rows
    total = jnp.zeros((1, 1), F32)
    row_id = lax.broadcasted_iota(jnp.int32, (cap, rows), 1).astype(F32)
    step_id = lax.broadcasted_iota(jnp.int32, (cap, rows), 0).astype(F32)
    for source in range(groups):
        theirs = owners[source][0:1, :]
        count = jnp.sum(jnp.where((theirs >= mine) & (theirs < mine + rows), 1.0, 0.0), axis=1, keepdims=True)
        hit = (row_id - step_id == total) & (step_id < count)
        place[pl.ds(source * cap, cap), :] = jnp.where(hit, 1.0, 0.0).astype(BF16)
        total = total + count
    live = jnp.where(lax.broadcasted_iota(jnp.int32, (rows, quarter), 0).astype(F32) < total, 1.0, 0.0)
    each(1, groups, lambda k: row_copy(k).wait())
    local[...] = dot(place[...], incoming[...].reshape(slots, quarter), TN).astype(BF16)
    whole[:, span(lane, quarter)] = local[...]
    whole_copies[0].start()
    whole_copies[1].start()
    cot_copies[0].wait_recv()
    cot_copies[2].start()
    whole_copies[0].wait_recv()
    whole_copies[2].start()

    def expand_on(k):
        expand_outer(k).wait_recv()
        expand_pair(k).start()

    each(1, outers, expand_on)
    project_pair(0).start()
    each(1, outers, lambda k: project_outer(k).start())

    for copies in (whole_copies,):
        copies[0].wait_send()
        copies[1].wait()
        copies[2].wait()
    floats = whole[...].astype(F32)
    row_mean = jnp.mean(floats, axis=1, keepdims=True)
    centred = floats - row_mean
    inv_scale = lax.rsqrt(jnp.mean(centred * centred, axis=1, keepdims=True) + EPS)
    scaled[...] = (centred * inv_scale * gain_ref[...]).astype(BF16)

    each(1, outers, lambda k: expand_outer(k).wait_send())
    each(0, outers, lambda k: expand_pair(k).wait())
    expand = flat(expand_full[...])
    joined = dot(scaled[...], expand)
    value[...] = joined[:, :quarter]
    gate[...] = sigmoid(joined[:, quarter:])

    def project_on(k):
        project_outer(k).wait_recv()
        project_pair(k).start()

    each(1, outers, project_on)
    edge = jnp.zeros((8, quarter), F32)
    around[0:8, :] = edge
    around[8 + rows:16 + rows, :] = edge
    around[8:8 + rows, :] = value[...] * gate[...]
    total_conv = jnp.zeros((rows, quarter), F32)
    for k in range(KSIZE):
        total_conv += taps_ref[k:k + 1, :] * around[8 - HALF + k:8 - HALF + k + rows, :] * mask_ref[:, k:k + 1]
    conv[...] = total_conv
    conv_sig = sigmoid(total_conv)
    hidden = (total_conv * conv_sig * live).astype(BF16)
    cot_copies[0].wait_send()
    cot_copies[1].wait()
    cot_copies[2].wait()
    project_terms[...] = dot(cot_full[...], hidden, TN).reshape(groups, depth, quarter).astype(BF16)
    each(1, outers, lambda k: gp_first(k).start())
    gp_first(0).start()

    each(1, outers, lambda k: project_outer(k).wait_send())
    each(0, outers, lambda k: project_pair(k).wait())
    project_back = flat(project_full[...])
    mixed_part[...] = dot(hidden, project_back, NT).astype(BF16)
    each(1, lanes, lambda k: mixed_copy(k).start())
    hidden_grad = dot(cot_full[...], project_back) * live
    conv_out = conv[...]
    conv_sig = sigmoid(conv_out)
    upstream[0:8, :] = edge
    upstream[8 + rows:16 + rows, :] = edge
    upstream[8:8 + rows, :] = hidden_grad * (conv_sig + conv_out * conv_sig * (1.0 - conv_sig))
    glu_grad = jnp.zeros((rows, quarter), F32)
    for k in range(KSIZE):
        glu_grad += (taps_ref[k:k + 1, :] * upstream[8 + HALF - k:8 + HALF - k + rows, :]
                     * mask_ref[:, KSIZE - 1 - k:KSIZE - k])
    gate_sig = gate[...]
    near = glu_grad * gate_sig
    proj_grad = jnp.concatenate([near.astype(BF16), (near * value[...] * (1.0 - gate_sig)).astype(BF16)], axis=1)
    expand_terms[...] = dot(scaled[...], proj_grad, TN).reshape(groups, depth, 2 * quarter).astype(BF16)
    each(1, outers, lambda k: ge_first(k).start())
    ge_first(0).start()
    scaled_part[...] = dot(proj_grad, expand, NT).astype(BF16)
    each(1, lanes, lambda k: scaled_copy(k).start())

    def project_term_on(k):
        gp_first(k).wait_recv()
        at = lax.rem(outer + k, outers)
        project_sum[at] = (project_terms[at * 2 + inner].astype(F32) + project_in[at].astype(F32)).astype(BF16)
        gp_second(k).start()

    def expand_term_on(k):
        ge_first(k).wait_recv()
        at = lax.rem(outer + k, outers)
        expand_sum[at] = (expand_terms[at * 2 + inner].astype(F32) + expand_in[at].astype(F32)).astype(BF16)
        ge_second(k).start()

    each(1, outers, project_term_on)
    small_out[...] = jnp.zeros(small_out.shape, F32)
    for k in range(KSIZE):
        small_out[k:k + 1, :] = jnp.sum(
            upstream[8:8 + rows, :] * around[8 - HALF + k:8 - HALF + k + rows, :] * mask_ref[:, k:k + 1],
            axis=0, keepdims=True)
    gp_first(0).wait_recv()
    grad_project_ref[...] = project_terms[me].astype(F32) + project_in[outer].astype(F32)
    expand_term_on(1)

    mixed_in[lane] = mixed_part[:, span(lane, quarter)]
    each(1, lanes, lambda k: mixed_copy(k).wait())
    mixed = mixed_in[0].astype(F32)
    for k in range(1, lanes):
        mixed = mixed + mixed_in[k].astype(F32)
    out_ref[...] = (local[...].astype(F32) + mixed).astype(BF16)

    scaled_in[lane] = scaled_part[:, span(lane, quarter)]
    each(1, lanes, lambda k: scaled_copy(k).wait())
    share = scaled_in[0].astype(F32)
    for k in range(1, lanes):
        share = share + scaled_in[k].astype(F32)
    normed = (local[...].astype(F32) - row_mean) * inv_scale
    grown = share * gain_local_ref[...]
    ones = jnp.ones((8, quarter), F32)
    sums_out[0:8, :] = dot(ones, grown, NT, lax.Precision.HIGHEST)
    sums_out[8:16, :] = dot(ones, grown * normed, NT, lax.Precision.HIGHEST)
    each(1, lanes, lambda k: sums_copy(k).start())
    small_out[KSIZE:KSIZE + 1, :] = jnp.sum(share * normed, axis=0, keepdims=True)
    each(1, groups, lambda k: small_copy(k).start())
    if outers > 2:
        expand_term_on(2)
    sums_in[lane] = sums_out[...]
    each(1, lanes, lambda k: sums_copy(k).wait())
    sums = sums_in[0]
    for k in range(1, lanes):
        sums = sums + sums_in[k]
    means = jnp.transpose(sums) * (1.0 / (lanes * quarter))
    back = inv_scale * (grown - means[:, 0:1] - normed * means[:, 8:9]) + cot_ref[...].astype(F32)
    returning[...] = dot(place[...], back.astype(BF16)).astype(BF16).reshape(groups, cap, quarter)
    each(1, groups, lambda k: back_copy(k).start())
    each(3, outers, expand_term_on)
    ge_first(0).wait_recv()
    grad_expand_ref[...] = expand_terms[me].astype(F32) + expand_in[outer].astype(F32)

    def project_add(k):
        gp_second(k).wait_recv()
        grad_project_ref[...] += project_last[lax.rem(outer - k + outers, outers)].astype(F32)

    each(1, outers, project_add)
    grad_project_ref[...] = grad_project_ref[...] * scale

    small_in[me] = small_out[...]
    each(1, groups, lambda k: small_copy(k).wait())
    small = small_in[0]
    for k in range(1, groups):
        small = small + small_in[k]
    small_ref[...] = small * scale

    returned[me] = returning[me]
    each(1, groups, lambda k: back_copy(k).wait())
    back_ref[...] = dot(pick[...], returned[...].reshape(slots, quarter), TN).astype(BF16)

    def expand_add(k):
        ge_second(k).wait_recv()
        grad_expand_ref[...] += expand_last[lax.rem(outer - k + outers, outers)].astype(F32)

    each(1, outers, expand_add)
    grad_expand_ref[...] = grad_expand_ref[...] * scale
    each(1, outers, lambda k: gp_second(k).wait_send())
    each(1, outers, lambda k: ge_second(k).wait_send())
    each(0, outers, lambda k: gp_first(k).wait_send())
    each(0, outers, lambda k: ge_first(k).wait_send())


def shards(frames, owner_slot, segment, norm_gain, expand, kernel, project, cotangent):
    rows, quarter = frames.shape
    groups, lanes = lax.axis_size("dp"), lax.axis_size("seq")
    lane = lax.axis_index("seq")
    cap = max(16, rows // groups)
    slots = groups * cap
    depth = D // groups
    outers = groups // 2
    inv_root = 1.0 / math.sqrt(rows * groups)
    vmem = pl.BlockSpec(memory_space=pltpu.VMEM)

    def sems(count):
        return pltpu.SemaphoreType.DMA((2, count))

    def terms(count, columns):
        return pltpu.VMEM((count, depth, columns), BF16)

    owner_rows = jnp.broadcast_to(owner_slot[None, :], (8, rows))
    labels = jnp.pad(segment[0], (HALF, HALF), constant_values=-1)
    masks = jnp.stack(
        [(labels[k : k + rows] == segment[0]).astype(F32) for k in range(KSIZE)] + [jnp.zeros((rows,), F32)] * (16 - KSIZE),
        axis=1,
    )
    gain_local = lax.dynamic_slice_in_dim(norm_gain, lane * quarter, quarter, 0)[None, :]
    share = pltpu.VMEM((rows, quarter), F32)
    padded = pltpu.VMEM((rows + 16, quarter), F32)
    all_columns = pltpu.VMEM((rows, D), BF16)
    buckets = pltpu.VMEM((groups, cap, quarter), BF16)
    lane_parts = pltpu.VMEM((lanes, rows, quarter), BF16)
    choice = pltpu.VMEM((slots, rows), BF16)
    output, grad_frames, small, grad_expand, grad_project = pl.pallas_call(
        functools.partial(block_kernel, groups, lanes, cap, inv_root),
        out_shape=(
            jax.ShapeDtypeStruct((rows, quarter), BF16),
            jax.ShapeDtypeStruct((rows, quarter), BF16),
            jax.ShapeDtypeStruct((16, quarter), F32),
            jax.ShapeDtypeStruct((depth, 2 * quarter), F32),
            jax.ShapeDtypeStruct((depth, quarter), F32),
        ),
        in_specs=[vmem] * 9,
        out_specs=(vmem,) * 5,
        scratch_shapes=[
            buckets, buckets, pltpu.VMEM((groups, 8, rows), jnp.int32), choice, choice,
            pltpu.VMEM((rows, quarter), BF16), all_columns, all_columns, all_columns,
            terms(groups, 2 * quarter), terms(groups, quarter),
            padded, padded, share, share, share, all_columns, all_columns,
            terms(groups, 2 * quarter), terms(outers, 2 * quarter), terms(outers, 2 * quarter), terms(outers, 2 * quarter),
            terms(groups, quarter), terms(outers, quarter), terms(outers, quarter), terms(outers, quarter),
            lane_parts, lane_parts,
            pltpu.VMEM((groups, 16, quarter), F32), pltpu.VMEM((16, quarter), F32),
            pltpu.VMEM((lanes, 16, rows), F32), pltpu.VMEM((16, rows), F32),
            buckets, buckets,
            sems(groups), sems(groups), sems(lanes), sems(lanes),
            sems(outers), sems(outers), sems(outers), sems(outers),
            sems(outers), sems(outers), sems(outers), sems(outers),
            sems(lanes), sems(lanes), sems(groups), sems(lanes), sems(groups),
        ],
        compiler_params=pltpu.CompilerParams(collective_id=0, has_side_effects=True, vmem_limit_bytes=58 << 20),
        name="conv_block",
    )(
        owner_rows, frames, expand.reshape(depth, 2 * quarter), project.T, cotangent,
        norm_gain[None, :], gain_local, kernel, masks,
    )
    return (
        output,
        grad_frames,
        small[KSIZE],
        small[:KSIZE],
        grad_expand.reshape(depth, 2, quarter),
        grad_project.T,
    )


def solution(mesh):
    placed = (
        P("dp", "seq"),
        P("dp"),
        P("dp", None),
        P(),
        P("dp", None, "seq"),
        P(None, "seq"),
        P("seq", "dp"),
        P("dp", "seq"),
    )
    return jax.shard_map(
        shards,
        mesh=mesh,
        in_specs=placed,
        out_specs=(
            P("dp", "seq"),
            P("dp", "seq"),
            P("seq"),
            P(None, "seq"),
            P("dp", None, "seq"),
            P("seq", "dp"),
        ),
        check_vma=False,
    )
```

```python
import functools
import math

import jax
import jax.numpy as jnp
from jax import lax
from jax.experimental import pallas as pl
from jax.experimental.pallas import tpu as pltpu
from jax.sharding import PartitionSpec as P

D = 1536
KSIZE = 9
HALF = KSIZE // 2
EPS = 1e-05
BF16 = jnp.bfloat16
F32 = jnp.float32
NT = (((1,), (1,)), ((), ()))
TN = (((0,), (0,)), ((), ()))


def dot(a, b, dims=(((1,), (0,)), ((), ())), precision=None):
    return lax.dot_general(a, b, dims, preferred_element_type=F32, precision=precision)


def span(index, size):
    return pl.ds(pl.multiple_of(index * size, size), size)


def enter(groups, lanes):
    me, lane = lax.axis_index("dp"), lax.axis_index("seq")
    barrier = pltpu.get_barrier_semaphore()

    def greet_group(k, carry):
        pl.semaphore_signal(barrier, inc=1, device_id=(lax.rem(me + k, groups), lane),
                            device_id_type=pl.DeviceIdType.MESH)
        return carry

    def greet_lane(k, carry):
        pl.semaphore_signal(barrier, inc=1, device_id=(me, lax.rem(lane + k, lanes)),
                            device_id_type=pl.DeviceIdType.MESH)
        return carry

    lax.fori_loop(1, groups, greet_group, 0)
    lax.fori_loop(1, lanes, greet_lane, 0)
    pl.semaphore_wait(barrier, groups + lanes - 2)


def remote(src, dst, sems, k, device):
    return pltpu.make_async_remote_copy(
        src_ref=src, dst_ref=dst, send_sem=sems.at[0, k], recv_sem=sems.at[1, k],
        device_id=device, device_id_type=pl.DeviceIdType.MESH)


def each(first, last, body):
    def step(k, carry):
        body(k)
        return carry

    lax.fori_loop(first, last, step, 0)


def flat(parts):
    n, rows, columns = parts.shape
    if rows % 16:
        return parts.astype(F32).reshape(n * rows, columns).astype(BF16)
    return parts.reshape(n * rows, columns)


def sigmoid(x):
    return 1.0 / (1.0 + jnp.exp(-x))


def block_kernel(groups, lanes, cap, scale,
                 owner_ref, segment_ref, frames_ref, expand_ref, project_ref, cot_ref, gain_ref, taps_ref,
                 out_ref, back_ref, small_ref, grad_expand_ref, grad_project_ref,
                 owner_out, labels, outgoing, incoming, owners, pick, place, local, whole, cot_full, scaled, weights,
                 around, upstream, conv, value, gate, mixed_part, scaled_part,
                 terms, terms_in, terms_sum, terms_last,
                 scaled_in, mixed_in, small_in, small_out, sums_in, sums_out, returning, returned,
                 owner_sem, row_sem, cot_sem, whole_sem, gather_outer_sem, gather_pair_sem,
                 term_pair_sem, term_outer_sem, scaled_sem, mixed_sem, small_sem, sums_sem, back_sem):
    rows, quarter = frames_ref.shape
    depth = expand_ref.shape[1]
    me, lane = lax.axis_index("dp"), lax.axis_index("seq")
    outers = groups // 2
    outer, inner = me // 2, lax.rem(me, 2)
    mate = outer * 2 + 1 - inner
    high, low = lane // 2, lax.rem(lane, 2)
    sibling = high * 2 + 1 - low
    opposite = lax.rem(lane + 2, lanes)
    slots = groups * cap
    owner_out[...] = jnp.broadcast_to(owner_ref[...], owner_out.shape)
    enter(groups, lanes)

    def to_group(src, dst, sems):
        def copy(k):
            return remote(src, dst.at[me], sems, k, (lax.rem(me + k, groups), lane))
        return copy

    def rows_to_group(src, dst, sems):
        def copy(k):
            to = lax.rem(me + k, groups)
            return remote(src.at[to], dst.at[me], sems, k, (to, lane))
        return copy

    def lane_gather(buffer, sems):
        own, far = buffer.at[:, span(lane, quarter)], buffer.at[:, span(opposite, quarter)]
        return (remote(own, own, sems, 0, (me, opposite)), remote(own, own, sems, 1, (me, sibling)),
                remote(far, far, sems, 2, (me, sibling)))

    def lane_scatter(src, dst, sems):
        def copy(k):
            to = lax.rem(lane + k, lanes)
            return remote(src.at[:, span(to, quarter)], dst.at[lane], sems, k, (me, to))
        return copy

    def gather_outer(u, k):
        part = weights.at[u, me]
        return remote(part, part, gather_outer_sem, u * outers + k, (lax.rem(outer + k, outers) * 2 + inner, lane))

    def gather_pair(u, k):
        part = weights.at[u, lax.rem(outer - k + outers, outers) * 2 + inner]
        return remote(part, part, gather_pair_sem, u * outers + k, (mate, lane))

    def term_pair(u, k):
        at = lax.rem(outer + k, outers)
        return remote(terms.at[u, at * 2 + 1 - inner], terms_in.at[u, at], term_pair_sem, u * outers + k, (mate, lane))

    def term_outer(u, k):
        at = lax.rem(outer + k, outers)
        return remote(terms_sum.at[u, at], terms_last.at[u, outer], term_outer_sem, u * outers + k,
                      (at * 2 + inner, lane))

    def gather_start(u):
        gather_pair(u, 0).start()
        each(1, outers, lambda k: gather_outer(u, k).start())

    def gather_on(u):
        def step(k):
            gather_outer(u, k).wait_recv()
            gather_pair(u, k).start()

        each(1, outers, step)

    def gather_end(u):
        each(1, outers, lambda k: gather_outer(u, k).wait_send())
        each(0, outers, lambda k: gather_pair(u, k).wait())

    def term_start(u, product):
        terms[u] = product.reshape(groups, depth, quarter).astype(BF16)
        each(1, outers, lambda k: term_pair(u, k).start())
        term_pair(u, 0).start()

    def term_on(u):
        def step(k):
            term_pair(u, k).wait_recv()
            at = lax.rem(outer + k, outers)
            terms_sum[u, at] = (terms[u, at * 2 + inner].astype(F32) + terms_in[u, at].astype(F32)).astype(BF16)
            term_outer(u, k).start()

        each(1, outers, step)
        term_pair(u, 0).wait_recv()

    def term_end(u):
        def step(k, total):
            term_outer(u, k).wait_recv()
            return total + terms_last[u, lax.rem(outer - k + outers, outers)].astype(F32)

        own = terms[u, me].astype(F32) + terms_in[u, outer].astype(F32)
        return lax.fori_loop(1, outers, step, own) * scale

    owner_copy = to_group(owner_out, owners, owner_sem)
    row_copy = rows_to_group(outgoing, incoming, row_sem)
    cot_copies = lane_gather(cot_full, cot_sem)
    whole_copies = lane_gather(whole, whole_sem)
    mixed_copy = lane_scatter(mixed_part, mixed_in, mixed_sem)
    scaled_copy = lane_scatter(scaled_part, scaled_in, scaled_sem)
    small_copy = to_group(small_out, small_in, small_sem)
    back_copy = rows_to_group(returning, returned, back_sem)

    def sums_copy(k):
        return remote(sums_out, sums_in.at[lane], sums_sem, k, (me, lax.rem(lane + k, lanes)))

    each(1, groups, lambda k: owner_copy(k).start())
    weights[0, me] = expand_ref[0]
    weights[1, me] = expand_ref[1]
    weights[2, me] = project_ref[...]
    gather_start(0)
    slot = owner_ref[0:1, :]
    group_id = lax.broadcasted_iota(jnp.int32, (groups, rows), 0)
    named = jnp.where((slot >= group_id * rows) & (slot < group_id * rows + rows), 1.0, 0.0)
    before = jnp.where(lax.broadcasted_iota(jnp.int32, (rows, rows), 0)
                       < lax.broadcasted_iota(jnp.int32, (rows, rows), 1), 1.0, 0.0).astype(BF16)
    rank = dot(named.astype(BF16), before)
    position = jnp.sum((rank + group_id.astype(F32) * cap + 1.0) * named, axis=0, keepdims=True) - 1.0
    pick[...] = jnp.where(lax.broadcasted_iota(jnp.int32, (slots, rows), 0) == position.astype(jnp.int32), 1.0, 0.0).astype(BF16)
    outgoing[...] = dot(pick[...], frames_ref[...]).astype(BF16).reshape(groups, cap, quarter)
    each(1, groups, lambda k: row_copy(k).start())
    gather_start(1)
    cot_full[:, span(lane, quarter)] = cot_ref[...]
    cot_copies[0].start()
    cot_copies[1].start()

    labels[0:8, :] = jnp.full((8, 128), -1.0, F32)
    labels[8 + rows:16 + rows, :] = jnp.full((8, 128), -1.0, F32)
    labels[8:8 + rows, :] = jnp.transpose(jnp.broadcast_to(segment_ref[...].astype(F32), (128, rows)))

    def mask(k):
        same = jnp.where(labels[8 - HALF + k:8 - HALF + k + rows, :] == labels[8:8 + rows, :], 1.0, 0.0)
        return jnp.concatenate([same] * (quarter // 128), axis=1)

    owners[me] = owner_out[...]
    incoming[me] = outgoing[me]
    each(1, groups, lambda k: owner_copy(k).wait())
    mine = lax.broadcasted_iota(jnp.int32, (1, rows), 1) * 0 + me * rows
    total = jnp.zeros((1, 1), F32)
    row_id = lax.broadcasted_iota(jnp.int32, (cap, rows), 1).astype(F32)
    step_id = lax.broadcasted_iota(jnp.int32, (cap, rows), 0).astype(F32)
    for source in range(groups):
        theirs = owners[source][0:1, :]
        count = jnp.sum(jnp.where((theirs >= mine) & (theirs < mine + rows), 1.0, 0.0), axis=1, keepdims=True)
        hit = (row_id - step_id == total) & (step_id < count)
        place[pl.ds(source * cap, cap), :] = jnp.where(hit, 1.0, 0.0).astype(BF16)
        total = total + count
    live = jnp.where(lax.broadcasted_iota(jnp.int32, (rows, quarter), 0).astype(F32) < total, 1.0, 0.0)
    gather_on(0)
    each(1, groups, lambda k: row_copy(k).wait())
    local[...] = dot(place[...], incoming[...].reshape(slots, quarter), TN).astype(BF16)
    whole[:, span(lane, quarter)] = local[...]
    whole_copies[0].start()
    whole_copies[1].start()
    gather_on(1)
    gather_start(2)
    whole_copies[0].wait_recv()
    whole_copies[2].start()
    cot_copies[0].wait_recv()
    cot_copies[2].start()
    for copies in (whole_copies,):
        copies[0].wait_send()
        copies[1].wait()
        copies[2].wait()
    floats = whole[...].astype(F32)
    row_mean = jnp.mean(floats, axis=1, keepdims=True)
    centred = floats - row_mean
    inv_scale = lax.rsqrt(jnp.mean(centred * centred, axis=1, keepdims=True) + EPS)
    scaled[...] = (centred * inv_scale * gain_ref[...]).astype(BF16)

    gather_end(0)
    expand_value = flat(weights[0])
    value[...] = dot(scaled[...], expand_value)
    gather_end(1)
    expand_gate = flat(weights[1])
    gate[...] = sigmoid(dot(scaled[...], expand_gate))
    gather_on(2)
    edge = jnp.zeros((8, quarter), F32)
    around[0:8, :] = edge
    around[8 + rows:16 + rows, :] = edge
    around[8:8 + rows, :] = value[...] * gate[...]
    total_conv = jnp.zeros((rows, quarter), F32)
    for k in range(KSIZE):
        total_conv += taps_ref[k:k + 1, :] * around[8 - HALF + k:8 - HALF + k + rows, :] * mask(k)
    conv[...] = total_conv
    conv_sig = sigmoid(total_conv)
    hidden = (total_conv * conv_sig * live).astype(BF16)
    cot_copies[0].wait_send()
    cot_copies[1].wait()
    cot_copies[2].wait()
    term_start(2, dot(cot_full[...], hidden, TN))
    gather_end(2)
    project_back = flat(weights[2])
    hidden_grad = dot(cot_full[...], project_back) * live
    conv_out = conv[...]
    conv_sig = sigmoid(conv_out)
    upstream[0:8, :] = edge
    upstream[8 + rows:16 + rows, :] = edge
    upstream[8:8 + rows, :] = hidden_grad * (conv_sig + conv_out * conv_sig * (1.0 - conv_sig))
    glu_grad = jnp.zeros((rows, quarter), F32)
    for k in range(KSIZE):
        glu_grad += (taps_ref[k:k + 1, :] * upstream[8 + HALF - k:8 + HALF - k + rows, :] * mask(KSIZE - 1 - k))
    gate_sig = gate[...]
    near = glu_grad * gate_sig
    value_grad = near.astype(BF16)
    gate_grad = (near * value[...] * (1.0 - gate_sig)).astype(BF16)
    term_start(0, dot(scaled[...], value_grad, TN))
    scaled_part[...] = (dot(value_grad, expand_value, NT) + dot(gate_grad, expand_gate, NT)).astype(BF16)
    each(1, lanes, lambda k: scaled_copy(k).start())
    term_start(1, dot(scaled[...], gate_grad, TN))
    term_on(2)
    mixed_part[...] = dot(hidden, project_back, NT).astype(BF16)
    each(1, lanes, lambda k: mixed_copy(k).start())
    small_out[...] = jnp.zeros(small_out.shape, F32)
    for k in range(KSIZE):
        small_out[k:k + 1, :] = jnp.sum(
            upstream[8:8 + rows, :] * around[8 - HALF + k:8 - HALF + k + rows, :] * mask(k),
            axis=0, keepdims=True)
    term_on(0)
    scaled_in[lane] = scaled_part[:, span(lane, quarter)]
    each(1, lanes, lambda k: scaled_copy(k).wait())
    share = scaled_in[0].astype(F32)
    for k in range(1, lanes):
        share = share + scaled_in[k].astype(F32)
    normed = (local[...].astype(F32) - row_mean) * inv_scale
    grown = share * gain_ref[:, span(lane, quarter)]
    ones = jnp.ones((8, quarter), F32)
    sums_out[0:8, :] = dot(ones, grown, NT, lax.Precision.HIGHEST)
    sums_out[8:16, :] = dot(ones, grown * normed, NT, lax.Precision.HIGHEST)
    each(1, lanes, lambda k: sums_copy(k).start())
    small_out[KSIZE:KSIZE + 1, :] = jnp.sum(share * normed, axis=0, keepdims=True)
    each(1, groups, lambda k: small_copy(k).start())
    sums_in[lane] = sums_out[...]
    each(1, lanes, lambda k: sums_copy(k).wait())
    sums = sums_in[0]
    for k in range(1, lanes):
        sums = sums + sums_in[k]
    means = jnp.transpose(sums) * (1.0 / (lanes * quarter))
    back = inv_scale * (grown - means[:, 0:1] - normed * means[:, 8:9]) + cot_ref[...].astype(F32)
    returning[...] = dot(place[...], back.astype(BF16)).astype(BF16).reshape(groups, cap, quarter)
    each(1, groups, lambda k: back_copy(k).start())
    term_on(1)
    mixed_in[lane] = mixed_part[:, span(lane, quarter)]
    each(1, lanes, lambda k: mixed_copy(k).wait())
    mixed = mixed_in[0].astype(F32)
    for k in range(1, lanes):
        mixed = mixed + mixed_in[k].astype(F32)
    out_ref[...] = (local[...].astype(F32) + mixed).astype(BF16)
    grad_project_ref[...] = term_end(2)

    small_in[me] = small_out[...]
    each(1, groups, lambda k: small_copy(k).wait())
    small = small_in[0]
    for k in range(1, groups):
        small = small + small_in[k]
    small_ref[...] = small * scale

    returned[me] = returning[me]
    each(1, groups, lambda k: back_copy(k).wait())
    back_ref[...] = dot(pick[...], returned[...].reshape(slots, quarter), TN).astype(BF16)

    grad_expand_ref[0] = term_end(0)
    grad_expand_ref[1] = term_end(1)
    for u in range(3):
        each(1, outers, lambda k: term_outer(u, k).wait_send())
        each(0, outers, lambda k: term_pair(u, k).wait_send())


def shards(frames, owner_slot, segment, norm_gain, expand, kernel, project, cotangent):
    rows, quarter = frames.shape
    groups, lanes = lax.axis_size("dp"), lax.axis_size("seq")
    cap = max(16, rows // groups)
    slots = groups * cap
    depth = D // groups
    outers = groups // 2
    inv_root = 1.0 / math.sqrt(rows * groups)
    vmem = pl.BlockSpec(memory_space=pltpu.VMEM)

    def sems(count):
        return pltpu.SemaphoreType.DMA((2, count))

    def terms(count):
        return pltpu.VMEM((3, count, depth, quarter), BF16)

    share = pltpu.VMEM((rows, quarter), F32)
    padded = pltpu.VMEM((rows + 16, quarter), F32)
    all_columns = pltpu.VMEM((rows, D), BF16)
    buckets = pltpu.VMEM((groups, cap, quarter), BF16)
    lane_parts = pltpu.VMEM((lanes, rows, quarter), BF16)
    choice = pltpu.VMEM((slots, rows), BF16)
    output, grad_frames, small, grad_expand, grad_project = pl.pallas_call(
        functools.partial(block_kernel, groups, lanes, cap, inv_root),
        out_shape=(
            jax.ShapeDtypeStruct((rows, quarter), BF16),
            jax.ShapeDtypeStruct((rows, quarter), BF16),
            jax.ShapeDtypeStruct((16, quarter), F32),
            jax.ShapeDtypeStruct((2, depth, quarter), F32),
            jax.ShapeDtypeStruct((depth, quarter), F32),
        ),
        in_specs=[vmem] * 8,
        out_specs=(vmem,) * 5,
        scratch_shapes=[
            pltpu.VMEM((8, rows), jnp.int32), pltpu.VMEM((rows + 16, 128), F32),
            buckets, buckets, pltpu.VMEM((groups, 8, rows), jnp.int32), choice, choice,
            pltpu.VMEM((rows, quarter), BF16), all_columns, all_columns, all_columns,
            terms(groups),
            padded, padded, share, share, share, all_columns, all_columns,
            terms(groups), terms(outers), terms(outers), terms(outers),
            lane_parts, lane_parts,
            pltpu.VMEM((groups, 16, quarter), F32), pltpu.VMEM((16, quarter), F32),
            pltpu.VMEM((lanes, 16, rows), F32), pltpu.VMEM((16, rows), F32),
            buckets, buckets,
            sems(groups), sems(groups), sems(lanes), sems(lanes),
            sems(3 * outers), sems(3 * outers), sems(3 * outers), sems(3 * outers),
            sems(lanes), sems(lanes), sems(groups), sems(lanes), sems(groups),
        ],
        compiler_params=pltpu.CompilerParams(collective_id=0, has_side_effects=True, vmem_limit_bytes=58 << 20),
        name="conv_block",
    )(
        owner_slot[None, :], segment, frames, expand.transpose(1, 0, 2), project.T, cotangent,
        norm_gain[None, :], kernel,
    )
    return (
        output,
        grad_frames,
        small[KSIZE],
        small[:KSIZE],
        grad_expand.transpose(1, 0, 2),
        grad_project.T,
    )


def solution(mesh):
    placed = (
        P("dp", "seq"),
        P("dp"),
        P("dp", None),
        P(),
        P("dp", None, "seq"),
        P(None, "seq"),
        P("seq", "dp"),
        P("dp", "seq"),
    )
    return jax.shard_map(
        shards,
        mesh=mesh,
        in_specs=placed,
        out_specs=(
            P("dp", "seq"),
            P("dp", "seq"),
            P("seq"),
            P(None, "seq"),
            P("dp", None, "seq"),
            P("seq", "dp"),
        ),
        check_vma=False,
    )
```
